512 devices in a mesh: gx: 32 (over z, core), gy: 16 (over x, y).
Axes of the slice: x: 4, y: 4, z: 16, core: 2. Of those that a mesh axis runs over, the one named last changes fastest.
Arguments:
- fields: float32 [4, 4, 4096, 2048], P(None, None, 'gx', 'gy'), may hold values from -6.5 to 6.5
- inv_dx: float32 [4096], P('gx'), may hold values from 0.5 to 2
- inv_dy: float32 [2048], P('gy'), may hold values from 0.5 to 2
Outputs:
- x_derivs: float32 [4, 4, 4096, 2048], P(None, None, 'gx', 'gy')
- y_derivs: float32 [4, 4, 4096, 2048], P(None, None, 'gx', 'gy')
The draws below stay inside these ranges and needn't reach their ends.
All inputs are finite; a program needn't handle non-finite values.
Results may differ from the reference program's by a relative error of at most 0.00013.
Values sent between devices are 32-bit elements; how exact they have to be, the bound alone decides.
A program may use at most 64 MiB of HBM per device.

```python
import math
import jax
import jax.numpy as jnp
from jax import lax

CZ = 4
NF = 4
NX = 4096
NY = 2048
COURANT = 256


def draw_fields(key, part):
    subkeys = jax.random.split(jax.random.fold_in(key, 7), 3)
    rough_part = jnp.clip(jax.random.normal(subkeys[0], (NF, CZ, NX, NY), jnp.float32), -4.0, 4.0)
    along_x = jnp.arange(NX).astype(jnp.float32) * (2.0 * jnp.pi / NX)
    along_y = jnp.arange(NY).astype(jnp.float32) * (2.0 * jnp.pi / NY)
    amplitude = jax.random.uniform(subkeys[1], (NF, CZ, 3, 2), jnp.float32, 0.1, 0.4)
    phases = jax.random.uniform(subkeys[2], (NF, CZ, 3, 2), jnp.float32, -jnp.pi, jnp.pi)
    wave_index = jnp.arange(1, 4).astype(jnp.float32)
    smooth_x = jnp.sum(amplitude[:, :, :, 0][..., None] * jnp.sin(wave_index[:, None] * along_x[None, :] + phases[:, :, :, 0][..., None]), axis=2)
    smooth_y = jnp.sum(amplitude[:, :, :, 1][..., None] * jnp.sin(wave_index[:, None] * along_y[None, :] + phases[:, :, :, 1][..., None]), axis=2)
    smooth_part = smooth_x[:, :, :, None] + smooth_y[:, :, None, :]
    return (rough_part + smooth_part).astype(jnp.float32)


def block_levels(stream_key, shape, cuts, smallest, largest):
    factor_of, own = 1.0, jax.random.fold_in(stream_key, 6)
    for dim, parts in cuts:
        draws = jnp.exp(jax.random.uniform(jax.random.fold_in(own, dim), (parts,), jnp.float32, smallest / len(cuts), largest / len(cuts)))
        factor_of = factor_of * jnp.repeat(draws, shape[dim] // parts).reshape([-1 if axis == dim else 1 for axis in range(len(shape))])
    return factor_of


def setup_inputs(seed: int = 0) -> dict:
    splits = jax.random.split(jax.random.key(seed), 4)
    return {
        "fields": draw_fields(jax.random.fold_in(splits[3], 71), 0),
        "inv_dx": jnp.clip(jnp.exp(math.log(2.0) - 1.3862944 * jax.random.uniform(splits[1], (NX,), jnp.float32) ** block_levels(splits[1], (NX,), ((0, 32),), -0.2, 0.2)), 0.5, 2.0),
        "inv_dy": jnp.clip(jnp.exp(math.log(2.0) - 1.3862944 * jax.random.uniform(splits[2], (NY,), jnp.float32) ** block_levels(splits[2], (NY,), ((0, 16),), -0.2, 0.2)), 0.5, 2.0),
    }


def implicit_line(single, line_axis):
    length = single.shape[line_axis]
    right_side = single + (4.0 / 9.0) * (jnp.roll(single, -1, line_axis) + jnp.roll(single, 1, line_axis)) + (1.0 / 36.0) * (jnp.roll(single, -2, line_axis) + jnp.roll(single, 2, line_axis))
    wavenum = jnp.arange(length // 2 + 1).astype(jnp.float32) * (2.0 * jnp.pi / length)
    left_symbol = 1.0 + 2.0 * (4.0 / 9.0) * jnp.cos(wavenum) + 2.0 * (1.0 / 36.0) * jnp.cos(2.0 * wavenum)
    odd_symbol = 2.0 * (20.0 / 27.0) * jnp.sin(wavenum) + 2.0 * (25.0 / 216.0) * jnp.sin(2.0 * wavenum)
    full_symbol = left_symbol + 1j * (COURANT * odd_symbol)
    shape_b = [1] * single.ndim
    shape_b[line_axis] = length // 2 + 1
    spectrum = jnp.fft.rfft(right_side, axis=line_axis)
    solved = jnp.fft.irfft(spectrum / full_symbol.reshape(shape_b), n=length, axis=line_axis)
    return solved.astype(jnp.float32)


def reference(fields, inv_dx, inv_dy):
    def one_field(single):
        along_x = (single - implicit_line(single, 1)) * inv_dx[None, :, None]
        along_y = (single - implicit_line(single, 2)) * inv_dy[None, None, :]
        return along_x, along_y

    x_derivs, y_derivs = lax.map(one_field, fields)
    return x_derivs, y_derivs
```

```python
import functools

import jax
import jax.numpy as jnp
import numpy as np
from jax import lax
from jax.experimental import pallas as pl
from jax.experimental.pallas import tpu as pltpu
from jax.sharding import PartitionSpec as P

MESH = pl.DeviceIdType.MESH
HIGHEST = lax.Precision.HIGHEST
F32 = jnp.float32
BETA = 1.0 / 36.0


def line_modes(courant):
    a, b = 4.0 / 9.0, BETA
    near, far = courant * 20.0 / 27.0, courant * 25.0 / 216.0
    top = np.array([b, a, 1.0, a, b])
    bottom = np.array([b + far, a + near, 1.0, a - near, b - far])
    roots = np.real(np.roots(bottom))
    for _ in range(4):
        roots = roots - np.polyval(bottom, roots) / np.polyval(np.polyder(bottom), roots)
    residues = np.polyval(top, roots) / np.polyval(np.polyder(bottom), roots)
    inside = sorted((k for k in range(4) if abs(roots[k]) < 1), key=lambda k: -abs(roots[k]))
    outside = sorted((k for k in range(4) if abs(roots[k]) > 1), key=lambda k: abs(roots[k]))
    forward = [(roots[k], residues[k]) for k in inside]
    backward = [(1.0 / roots[k], residues[k]) for k in outside]
    return top[0] / bottom[0], forward, backward


def tables(n, courant):
    constant, forward, backward = line_modes(courant)
    lag = np.arange(n)[:, None] - np.arange(n)[None, :]
    local = np.zeros((n, n))
    for w, r in forward:
        local += np.where(lag >= 1, r * np.power(w, np.maximum(lag - 1, 0)), 0.0)
    for v, r in backward:
        local -= np.where(lag <= 0, r * np.power(v, np.maximum(1 - lag, 0)), 0.0)
    local += constant * np.eye(n)
    i = np.arange(n)
    (w1, r1), (w3, r3) = forward
    (v2, r2), (v4, r4) = backward
    source = np.stack([r1 * w1 ** (n - 1 - i), -r2 * v2 ** (i + 2), r3 * w3 ** (n - 1 - i), -r4 * v4 ** (i + 2)])
    response = np.stack([w1**i, v2 ** (n - 1 - i), w3**i, v4 ** (n - 1 - i)])
    return local, source, response, w1**n, v2**n


def tiny_off(array):
    out = np.asarray(array, np.float32)
    return np.where(np.abs(out) < np.finfo(np.float32).tiny, np.float32(0), out)


def wait_bytes(ref, sem):
    pltpu.make_async_copy(ref, ref, sem).wait()


def exchange_kernel(q1, q2, nz, ny, planes, n,
                    fields, inv_x, inv_y, consts,
                    x_out, y_out,
                    f, cst, ixv, iyv, pre_y, coef, sx, px, pbuf, rb, gbuf, gpar, fast, sy, yb, yn,
                    load_sem, pair_s, pair_r, fast_s, fast_r, far_s, far_r, ret_s, ret_r,
                    ys_s, ys_r, yn_s, yn_r):
    gx, gy = lax.axis_index("gx"), lax.axis_index("gy")
    c, z = lax.rem(gx, 2), lax.div(gx, 2)
    half = planes // 2
    chunks = 4
    step = planes // chunks
    loads = []
    for k in range(chunks):
        loads.append(pltpu.make_async_copy(fields.at[pl.ds(k * step, step)], f.at[pl.ds(k * step, step)], load_sem.at[k]))
    loads.append(pltpu.make_async_copy(consts, cst, load_sem.at[chunks]))
    loads.append(pltpu.make_async_copy(inv_x, ixv, load_sem.at[chunks + 1]))
    loads.append(pltpu.make_async_copy(inv_y, iyv, load_sem.at[chunks + 2]))
    loads[chunks].start()
    for k in range(chunks):
        loads[k].start()
    loads[chunks + 1].start()
    loads[chunks + 2].start()

    def chip(m):
        return (lax.rem(gx + 2 * m, 2 * nz), gy)

    def along_y(m):
        return (gx, lax.rem(gy + m, ny))

    partner = (gx + 1 - 2 * c, gy)
    beside = (lax.rem(gx + 2 * nz - 1 + 2 * c, 2 * nz), gy)

    barrier = pltpu.get_barrier_semaphore()
    greeted = [chip(m) for m in range(1, nz)] + [partner, beside] + [along_y(m) for m in range(1, ny)]
    for d in greeted:
        pl.semaphore_signal(barrier, inc=1, device_id=d, device_id_type=MESH)

    loads[chunks].wait()
    row32 = lax.broadcasted_iota(jnp.int32, (32, n), 0)
    wsrc = cst[pl.ds(n, 32)]
    for h in range(2):
        acc = jnp.zeros((32, n), F32)
        for p in range(half):
            fz = h * half + p
            if fz % step == 0:
                loads[fz // step].wait()
            w = jnp.where(lax.rem(row32, half) == p, wsrc, 0.0)
            acc = acc + jnp.dot(w, f[fz], preferred_element_type=F32, precision=HIGHEST)
        for k in range(4):
            sx[k, h] = acc[k * half:(k + 1) * half]

    pl.semaphore_wait(barrier, len(greeted))

    pair = pltpu.make_async_remote_copy(sx, px, pair_s, pair_r, device_id=partner, device_id_type=MESH)
    pair.start()
    side = pltpu.make_async_remote_copy(sx.at[3 - c], fast, fast_s, fast_r, device_id=beside, device_id_type=MESH)
    side.start()
    pair.wait_recv()
    first = c == 0
    pbuf[0] = jnp.where(first, q1, 1.0) * sx[0, c] + jnp.where(first, 1.0, q1) * px[0, c]
    pbuf[1] = jnp.where(first, 1.0, q2) * sx[1, c] + jnp.where(first, q2, 1.0) * px[1, c]
    for zd in range(nz):
        @pl.when(z != zd)
        def _():
            slot = lax.rem(zd - z + nz, nz)
            pltpu.make_async_remote_copy(
                pbuf, rb.at[slot], far_s, far_r, device_id=(2 * zd + c, gy), device_id_type=MESH).start()

    for h in range(2):
        acc = jnp.zeros((32, n), F32)
        for p in range(half):
            w = jnp.where(lax.rem(row32, half) == p, wsrc, 0.0)
            acc = acc + lax.dot_general(w, f[h * half + p], (((1,), (1,)), ((), ())),
                                        preferred_element_type=F32, precision=HIGHEST)
        for k in range(4):
            sy[k, h] = acc[k * half:(k + 1) * half]
    for m in range(1, ny):
        pltpu.make_async_remote_copy(
            sy.at[pl.ds(0, 2)], yb.at[m], ys_s, ys_r, device_id=along_y(m), device_id_type=MESH).start()
    beyond = []
    for k, m in ((0, 1), (1, ny - 1)):
        copy = pltpu.make_async_remote_copy(
            sy.at[2 + k], yn.at[k], yn_s.at[k], yn_r.at[k], device_id=along_y(m), device_id_type=MESH)
        copy.start()
        beyond.append(copy)

    loads[chunks + 1].wait()
    loads[chunks + 2].wait()
    ix = jnp.transpose(jnp.broadcast_to(ixv[...], (n, n)))
    iy = iyv[...]
    for k in range(4):
        coef[k] = cst[pl.ds(n + 96, n), pl.ds(k, 1)] * ix
    coef[4] = ix
    local = cst[pl.ds(0, n)]

    def plane(fz, carry):
        cells = f[fz]
        x_out[fz] = (cells - jnp.dot(local, cells, preferred_element_type=F32, precision=HIGHEST)) * coef[4]
        y_line = lax.dot_general(cells, local, (((1,), (1,)), ((), ())), preferred_element_type=F32, precision=HIGHEST)
        pre_y[fz] = (cells - y_line) * iy
        return carry

    lax.fori_loop(0, planes, plane, 0)

    wait_bytes(yb.at[pl.ds(1, ny - 1)], ys_r)
    close1, close2 = 1.0 / (1.0 - q1**ny), 1.0 / (1.0 - q2**ny)
    fy1 = (close1 * q1 ** (ny - 1)) * sy[0]
    fy2 = (close2 * q2 ** (ny - 1)) * sy[1]
    for m in range(1, ny):
        fy1 = fy1 + (close1 * q1 ** (m - 1)) * yb[m, 0]
        fy2 = fy2 + (close2 * q2 ** (ny - m - 1)) * yb[m, 1]
    beyond[0].wait_recv()
    beyond[1].wait_recv()
    fy = jnp.concatenate([fy1.reshape(planes, n), fy2.reshape(planes, n), yn[0].reshape(planes, n),
                          yn[1].reshape(planes, n), jnp.zeros((n - 4 * planes, n), F32)], axis=0)
    fyt = jnp.transpose(fy)
    back = cst[pl.ds(n + 32, 64)] * iy
    back = jnp.concatenate([back, jnp.zeros((n - 4 * planes, n), F32)], axis=0)
    rown = lax.broadcasted_iota(jnp.int32, (n, n), 0)

    def y_plane(fz, carry):
        rhs = jnp.where(lax.rem(rown, planes) == fz, back, 0.0)
        y_out[fz] = pre_y[fz] - jnp.dot(fyt, rhs, preferred_element_type=F32, precision=HIGHEST)
        return carry

    lax.fori_loop(0, planes, y_plane, 0)

    wait_bytes(rb.at[pl.ds(1, nz - 1)], far_r)
    e1, e2 = q1 * q1, q2 * q2
    close1, close2 = 1.0 / (1.0 - e1**nz), 1.0 / (1.0 - e2**nz)
    g1 = (close1 * e1 ** (nz - 1)) * pbuf[0]
    g2 = (close2 * e2 ** (nz - 1)) * pbuf[1]
    for m in range(1, nz):
        g1 = g1 + (close1 * e1 ** (m - 1)) * rb[m, 0]
        g2 = g2 + (close2 * e2 ** (nz - m - 1)) * rb[m, 1]
    gbuf[0] = g1
    gbuf[1] = g2
    ret = pltpu.make_async_remote_copy(gbuf, gpar, ret_s, ret_r, device_id=partner, device_id_type=MESH)
    ret.start()
    side.wait_recv()
    a1 = jnp.where(first, 1.0, q1)
    b1 = jnp.where(first, 0.0, 1.0)
    a2 = jnp.where(first, q2, 1.0)
    b2 = jnp.where(first, 1.0, 0.0)
    f3 = jnp.where(first, fast[...], px[2])
    f4 = jnp.where(first, px[3], fast[...])
    ret.wait_recv()
    own1, own2, par1, par2 = gbuf[0], gbuf[1], gpar[0], gpar[1]
    for h in range(2):
        mine = c == h
        f1 = a1 * jnp.where(mine, own1, par1) + b1 * px[0, h]
        f2 = a2 * jnp.where(mine, own2, par2) + b2 * px[1, h]
        for p in range(half):
            fz = h * half + p
            fix = coef[0] * f1[p:p + 1] + coef[1] * f2[p:p + 1]
            x_out[fz] = x_out[fz] - fix - coef[2] * f3[h, p:p + 1] - coef[3] * f4[h, p:p + 1]

    pair.wait_send()
    side.wait_send()
    ret.wait_send()
    beyond[0].wait_send()
    beyond[1].wait_send()
    wait_bytes(rb.at[pl.ds(1, nz - 1)], far_s)
    wait_bytes(yb.at[pl.ds(1, ny - 1)], ys_s)


def store_kernel(x_in, y_in, x_out, y_out, sem):
    copies = [pltpu.make_async_copy(x_in, x_out, sem.at[0]), pltpu.make_async_copy(y_in, y_out, sem.at[1])]
    for copy in copies:
        copy.start()
    for copy in copies:
        copy.wait()


def on_device(fields, inv_dx, inv_dy):
    nfield, nplane, n, ncol = fields.shape
    gxn, gyn = lax.axis_size("gx"), lax.axis_size("gy")
    planes, nz = nfield * nplane, gxn // 2
    courant = float(n * gxn // 16)
    local, source, response, q1, q2 = tables(n, courant)
    half = planes // 2
    consts = np.concatenate([
        local,
        np.repeat(source, half, axis=0),
        np.repeat(response, planes, axis=0),
        np.pad(response.T, ((0, 0), (0, n - 4))),
    ], axis=0)
    consts = jnp.asarray(tiny_off(consts))
    block = jax.ShapeDtypeStruct((planes, n, n), F32)
    hbm = pl.BlockSpec(memory_space=pltpu.HBM)
    vmem = pl.BlockSpec(memory_space=pltpu.VMEM)
    vm = lambda *shape: pltpu.VMEM(shape, F32)
    dma = pltpu.SemaphoreType.DMA
    x_pre, y_pre = pl.pallas_call(
        functools.partial(exchange_kernel, float(q1), float(q2), nz, gyn, planes, n),
        out_shape=(pltpu.VMEM((planes, n, n), F32), pltpu.VMEM((planes, n, n), F32)),
        in_specs=[hbm] * 4,
        out_specs=(vmem, vmem),
        scratch_shapes=[
            vm(planes, n, n), vm(*consts.shape), vm(1, n), vm(1, n), vm(planes, n, n), vm(5, n, n),
            vm(4, 2, half, n), vm(4, 2, half, n), vm(2, half, n), vm(nz, 2, half, n), vm(2, half, n), vm(2, half, n),
            vm(2, half, n), vm(4, 2, half, n), vm(gyn, 2, 2, half, n), vm(2, 2, half, n),
            dma((7,)), dma, dma, dma, dma, dma, dma, dma, dma, dma, dma, dma((2,)), dma((2,)),
        ],
        compiler_params=pltpu.CompilerParams(
            collective_id=0, has_side_effects=True, vmem_limit_bytes=24 * 1024 * 1024),
        name="exchange",
    )(*(pltpu.with_memory_space_constraint(a, pltpu.HBM)
        for a in (fields.reshape(planes, n, n), inv_dx.reshape(1, n), inv_dy.reshape(1, n), consts)))
    x_derivs, y_derivs = pl.pallas_call(
        store_kernel,
        out_shape=(block, block),
        in_specs=[vmem, vmem],
        out_specs=(hbm, hbm),
        scratch_shapes=[dma((2,))],
        compiler_params=pltpu.CompilerParams(vmem_limit_bytes=24 * 1024 * 1024),
        name="store",
    )(x_pre, y_pre)
    return x_derivs.reshape(fields.shape), y_derivs.reshape(fields.shape)


def solution(mesh):
    spec = P(None, None, "gx", "gy")
    return jax.shard_map(
        on_device, mesh=mesh, in_specs=(spec, P("gx"), P("gy")), out_specs=(spec, spec), check_vma=False
    )
```

```python
import functools

import jax
import jax.numpy as jnp
import numpy as np
from jax import lax
from jax.experimental import pallas as pl
from jax.experimental.pallas import tpu as pltpu
from jax.sharding import PartitionSpec as P

MESH = pl.DeviceIdType.MESH
HIGHEST = lax.Precision.HIGHEST
F32 = jnp.float32
BETA = 1.0 / 36.0


def line_modes(courant):
    a, b = 4.0 / 9.0, BETA
    near, far = courant * 20.0 / 27.0, courant * 25.0 / 216.0
    top = np.array([b, a, 1.0, a, b])
    bottom = np.array([b + far, a + near, 1.0, a - near, b - far])
    roots = np.real(np.roots(bottom))
    for _ in range(4):
        roots = roots - np.polyval(bottom, roots) / np.polyval(np.polyder(bottom), roots)
    residues = np.polyval(top, roots) / np.polyval(np.polyder(bottom), roots)
    inside = sorted((k for k in range(4) if abs(roots[k]) < 1), key=lambda k: -abs(roots[k]))
    outside = sorted((k for k in range(4) if abs(roots[k]) > 1), key=lambda k: abs(roots[k]))
    forward = [(roots[k], residues[k]) for k in inside]
    backward = [(1.0 / roots[k], residues[k]) for k in outside]
    return top[0] / bottom[0], forward, backward


def tables(n, courant):
    constant, forward, backward = line_modes(courant)
    lag = np.arange(n)[:, None] - np.arange(n)[None, :]
    local = np.zeros((n, n))
    for w, r in forward:
        local += np.where(lag >= 1, r * np.power(w, np.maximum(lag - 1, 0)), 0.0)
    for v, r in backward:
        local -= np.where(lag <= 0, r * np.power(v, np.maximum(1 - lag, 0)), 0.0)
    local += constant * np.eye(n)
    i = np.arange(n)
    (w1, r1), (w3, r3) = forward
    (v2, r2), (v4, r4) = backward
    source = np.stack([r1 * w1 ** (n - 1 - i), -r2 * v2 ** (i + 2), r3 * w3 ** (n - 1 - i), -r4 * v4 ** (i + 2)])
    response = np.stack([w1**i, v2 ** (n - 1 - i), w3**i, v4 ** (n - 1 - i)])
    return local, source, response, w1**n, v2**n


def tiny_off(array):
    out = np.asarray(array, np.float32)
    return np.where(np.abs(out) < np.finfo(np.float32).tiny, np.float32(0), out)


def wait_bytes(ref, sem):
    pltpu.make_async_copy(ref, ref, sem).wait()


def exchange_kernel(q1, q2, nz, ny, planes, n,
                    fields, inv_x, inv_y, consts,
                    x_out, y_out,
                    f, cst, ixv, iyv, pre_y, coef, back, sx, px, pbuf, rb, gbuf, gpar, fast, sy, yb, yn,
                    load_sem, pair_s, pair_r, fast_s, fast_r, far_s, far_r, ret_s, ret_r,
                    ys_s, ys_r, yn_s, yn_r, ready, relay):
    gx, gy = lax.axis_index("gx"), lax.axis_index("gy")
    c, z = lax.rem(gx, 2), lax.div(gx, 2)
    half, low = planes // 2, nz // 2
    early, late = z < low, z >= low
    chunks = 4
    step = planes // chunks
    loads = [pltpu.make_async_copy(consts, cst, load_sem.at[chunks])]
    for k in range(chunks):
        loads.append(pltpu.make_async_copy(fields.at[pl.ds(k * step, step)], f.at[pl.ds(k * step, step)], load_sem.at[k]))
    loads.append(pltpu.make_async_copy(inv_x, ixv, load_sem.at[chunks + 1]))
    loads.append(pltpu.make_async_copy(inv_y, iyv, load_sem.at[chunks + 2]))
    for load in loads:
        load.start()

    def chip(m):
        return (lax.rem(gx + 2 * m, 2 * nz), gy)

    def along_y(m):
        return (gx, lax.rem(gy + m, ny))

    def signal(sem, device):
        pl.semaphore_signal(sem, inc=1, device_id=device, device_id_type=MESH)

    partner = (gx + 1 - 2 * c, gy)
    beside = (lax.rem(gx + 2 * nz - 1 + 2 * c, 2 * nz), gy)

    barrier = pltpu.get_barrier_semaphore()
    signal(barrier, partner)
    signal(barrier, beside)

    @pl.when(early)
    def _():
        for m in range(1, nz):
            signal(barrier, chip(m))

    for m in range(1, ny):
        signal(barrier, along_y(m))

    def x_sources():
        rows = n + 32 + 64 + n
        w1, w2 = cst.at[pl.ds(rows, n)], cst.at[pl.ds(rows + n, n)]
        w3, w4 = cst.at[pl.ds(rows + 2 * n, n // 2)], cst.at[pl.ds(rows + 2 * n + n // 2, n // 2)]

        def total(v):
            return jnp.sum(jnp.sum(v.reshape(-1, 8, n), axis=0), axis=0, keepdims=True)

        loads[0].wait()
        for fz in range(planes):
            if fz % step == 0:
                loads[1 + fz // step].wait()
            cells = f[fz]
            h, p = fz // half, fz % half
            sx[0, h, p:p + 1] = total(cells * w1[...])
            sx[1, h, p:p + 1] = total(cells * w2[...])
            sx[2, h, p:p + 1] = total(cells[n // 2:] * w3[...])
            sx[3, h, p:p + 1] = total(cells[:n // 2] * w4[...])

    def y_sources():
        row32 = lax.broadcasted_iota(jnp.int32, (32, n), 0)
        wsrc = cst[pl.ds(n, 32)]
        for h in range(2):
            acc = jnp.zeros((32, n), F32)
            for p in range(half):
                w = jnp.where(lax.rem(row32, half) == p, wsrc, 0.0)
                acc = acc + lax.dot_general(w, f[h * half + p], (((1,), (1,)), ((), ())),
                                            preferred_element_type=F32, precision=HIGHEST)
            for k in range(4):
                sy[k, h] = acc[k * half:(k + 1) * half]

    def local_products():
        loads[chunks + 1].wait()
        loads[chunks + 2].wait()
        ix = jnp.transpose(jnp.broadcast_to(ixv[...], (n, n)))
        iy = iyv[...]
        for k in range(4):
            coef[k] = cst[pl.ds(n + 96, n), pl.ds(k, 1)] * ix
        coef[4] = ix
        local = cst[pl.ds(0, n)]
        answer = cst[pl.ds(n + 32, 4 * planes)] * iy
        top = answer.astype(jnp.bfloat16).astype(F32)
        rest = answer - top
        row = lax.rem(lax.broadcasted_iota(jnp.int32, (4 * planes, n), 0), planes)

        def plane(fz, carry):
            cells = f[fz]
            x_line = jnp.dot(local, cells, preferred_element_type=F32, precision=HIGHEST)
            x_out[fz] = (cells - x_line) * coef[4]
            y_line = lax.dot_general(cells, local, (((1,), (1,)), ((), ())),
                                     preferred_element_type=F32, precision=HIGHEST)
            pre_y[fz] = (cells - y_line) * iy
            one = jnp.where(row == fz, top, 0.0).astype(jnp.bfloat16)
            two = jnp.where(row == fz, rest, 0.0).astype(jnp.bfloat16)
            back[fz] = jnp.concatenate([one, two, one, two], axis=0)
            return carry

        lax.fori_loop(0, planes, plane, 0, unroll=4)

    def far_sends(chips):
        for zd in chips:
            @pl.when(z != zd)
            def _():
                pltpu.make_async_remote_copy(
                    pbuf, rb.at[lax.rem(zd - z + nz, nz)], far_s, far_r,
                    device_id=(2 * zd + c, gy), device_id_type=MESH).start()

    def y_sends():
        for m in range(1, ny):
            pltpu.make_async_remote_copy(
                sy.at[pl.ds(0, 2)], yb.at[m], ys_s, ys_r, device_id=along_y(m), device_id_type=MESH).start()
        for copy in beyond:
            copy.start()

    beyond = [
        pltpu.make_async_remote_copy(
            sy.at[2 + k], yn.at[k], yn_s.at[k], yn_r.at[k], device_id=along_y(m), device_id_type=MESH)
        for k, m in ((0, 1), (1, ny - 1))
    ]

    x_sources()

    @pl.when(early)
    def _():
        y_sources()
        local_products()

    pl.semaphore_wait(barrier, jnp.where(early, low - 1, low) + 2 + ny - 1)

    pair = pltpu.make_async_remote_copy(sx, px, pair_s, pair_r, device_id=partner, device_id_type=MESH)
    pair.start()

    @pl.when(late)
    def _():
        for zd in range(low):
            signal(ready, (2 * zd + c, gy))

    side = pltpu.make_async_remote_copy(sx.at[3 - c], fast, fast_s, fast_r, device_id=beside, device_id_type=MESH)
    side.start()
    pair.wait_recv()
    first = c == 0
    pbuf[0] = jnp.where(first, q1, 1.0) * sx[0, c] + jnp.where(first, 1.0, q1) * px[0, c]
    pbuf[1] = jnp.where(first, 1.0, q2) * sx[1, c] + jnp.where(first, q2, 1.0) * px[1, c]
    far_sends(range(low))

    @pl.when(late)
    def _():
        y_sources()
        y_sends()
        local_products()
        pl.semaphore_wait(relay, 1)

    @pl.when(early)
    def _():
        y_sends()
        pl.semaphore_wait(ready, nz - low)
        signal(relay, (2 * (nz - 1 - z) + c, gy))

    far_sends(range(low, nz))

    wait_bytes(yb.at[pl.ds(1, ny - 1)], ys_r)
    close1, close2 = 1.0 / (1.0 - q1**ny), 1.0 / (1.0 - q2**ny)
    fy1 = (close1 * q1 ** (ny - 1)) * sy[0]
    fy2 = (close2 * q2 ** (ny - 1)) * sy[1]
    for m in range(1, ny):
        fy1 = fy1 + (close1 * q1 ** (m - 1)) * yb[m, 0]
        fy2 = fy2 + (close2 * q2 ** (ny - m - 1)) * yb[m, 1]
    beyond[0].wait_recv()
    beyond[1].wait_recv()
    fy = jnp.concatenate([v.reshape(planes, n) for v in (fy1, fy2, yn[0], yn[1])], axis=0)
    top = fy.astype(jnp.bfloat16).astype(F32)
    rest = fy - top
    lhs = jnp.concatenate([jnp.transpose(jnp.concatenate([v, v], axis=0)) for v in (top, rest)], axis=1).astype(jnp.bfloat16)
    for fz in range(planes):
        y_out[fz] = pre_y[fz] - jnp.dot(lhs, back[fz], preferred_element_type=F32)

    wait_bytes(rb.at[pl.ds(1, nz - 1)], far_r)
    e1, e2 = q1 * q1, q2 * q2
    close1, close2 = 1.0 / (1.0 - e1**nz), 1.0 / (1.0 - e2**nz)
    g1 = (close1 * e1 ** (nz - 1)) * pbuf[0]
    g2 = (close2 * e2 ** (nz - 1)) * pbuf[1]
    for m in range(1, nz):
        g1 = g1 + (close1 * e1 ** (m - 1)) * rb[m, 0]
        g2 = g2 + (close2 * e2 ** (nz - m - 1)) * rb[m, 1]
    gbuf[0] = g1
    gbuf[1] = g2
    ret = pltpu.make_async_remote_copy(gbuf, gpar, ret_s, ret_r, device_id=partner, device_id_type=MESH)
    ret.start()
    side.wait_recv()
    a1 = jnp.where(first, 1.0, q1)
    b1 = jnp.where(first, 0.0, 1.0)
    a2 = jnp.where(first, q2, 1.0)
    b2 = jnp.where(first, 1.0, 0.0)
    f3 = jnp.where(first, fast[...], px[2])
    f4 = jnp.where(first, px[3], fast[...])
    pair.wait_send()
    side.wait_send()
    beyond[0].wait_send()
    beyond[1].wait_send()
    wait_bytes(rb.at[pl.ds(1, nz - 1)], far_s)
    wait_bytes(yb.at[pl.ds(1, ny - 1)], ys_s)
    ret.wait_recv()
    own1, own2, par1, par2 = gbuf[0], gbuf[1], gpar[0], gpar[1]
    for h in range(2):
        mine = c == h
        f1 = a1 * jnp.where(mine, own1, par1) + b1 * px[0, h]
        f2 = a2 * jnp.where(mine, own2, par2) + b2 * px[1, h]
        for p in range(half):
            fz = h * half + p
            fix = coef[0] * f1[p:p + 1] + coef[1] * f2[p:p + 1]
            x_out[fz] = x_out[fz] - fix - coef[2] * f3[h, p:p + 1] - coef[3] * f4[h, p:p + 1]
    ret.wait_send()


def store_kernel(x_in, y_in, x_out, y_out, sem):
    parts = 4
    rows = x_in.shape[0] // parts
    copies = []
    for k in range(parts):
        part = pl.ds(k * rows, rows)
        copies.append(pltpu.make_async_copy(x_in.at[part], x_out.at[part], sem.at[2 * k]))
        copies.append(pltpu.make_async_copy(y_in.at[part], y_out.at[part], sem.at[2 * k + 1]))
    for copy in copies:
        copy.start()
    for copy in copies:
        copy.wait()


def on_device(fields, inv_dx, inv_dy):
    nfield, nplane, n, ncol = fields.shape
    gxn, gyn = lax.axis_size("gx"), lax.axis_size("gy")
    planes, nz = nfield * nplane, gxn // 2
    courant = float(n * gxn // 16)
    local, source, response, q1, q2 = tables(n, courant)
    half = planes // 2
    consts = np.concatenate([
        local,
        np.repeat(source, half, axis=0),
        np.repeat(response, planes, axis=0),
        np.pad(response.T, ((0, 0), (0, n - 4))),
        np.repeat(np.concatenate([source[0], source[1], source[2, n // 2:], source[3, :n // 2]])[:, None], n, axis=1),
    ], axis=0)
    consts = jnp.asarray(tiny_off(consts))
    block = jax.ShapeDtypeStruct((planes, n, n), F32)
    hbm = pl.BlockSpec(memory_space=pltpu.HBM)
    vmem = pl.BlockSpec(memory_space=pltpu.VMEM)
    vm = lambda *shape: pltpu.VMEM(shape, F32)
    dma = pltpu.SemaphoreType.DMA
    x_pre, y_pre = pl.pallas_call(
        functools.partial(exchange_kernel, float(q1), float(q2), nz, gyn, planes, n),
        out_shape=(pltpu.VMEM((planes, n, n), F32), pltpu.VMEM((planes, n, n), F32)),
        in_specs=[hbm] * 4,
        out_specs=(vmem, vmem),
        scratch_shapes=[
            vm(planes, n, n), vm(*consts.shape), vm(1, n), vm(1, n), vm(planes, n, n), vm(5, n, n),
            pltpu.VMEM((planes, 16 * planes, n), jnp.bfloat16),
            vm(4, 2, half, n), vm(4, 2, half, n), vm(2, half, n), vm(nz, 2, half, n), vm(2, half, n), vm(2, half, n),
            vm(2, half, n), vm(4, 2, half, n), vm(gyn, 2, 2, half, n), vm(2, 2, half, n),
            dma((7,)), dma, dma, dma, dma, dma, dma, dma, dma, dma, dma, dma((2,)), dma((2,)),
            pltpu.SemaphoreType.REGULAR, pltpu.SemaphoreType.REGULAR,
        ],
        compiler_params=pltpu.CompilerParams(
            collective_id=0, has_side_effects=True, vmem_limit_bytes=24 * 1024 * 1024),
        name="exchange",
    )(*(pltpu.with_memory_space_constraint(a, pltpu.HBM)
        for a in (fields.reshape(planes, n, n), inv_dx.reshape(1, n), inv_dy.reshape(1, n), consts)))
    x_derivs, y_derivs = pl.pallas_call(
        store_kernel,
        out_shape=(block, block),
        in_specs=[vmem, vmem],
        out_specs=(hbm, hbm),
        scratch_shapes=[dma((8,))],
        compiler_params=pltpu.CompilerParams(vmem_limit_bytes=24 * 1024 * 1024),
        name="store",
    )(x_pre, y_pre)
    return x_derivs.reshape(fields.shape), y_derivs.reshape(fields.shape)


def solution(mesh):
    spec = P(None, None, "gx", "gy")
    return jax.shard_map(
        on_device, mesh=mesh, in_specs=(spec, P("gx"), P("gy")), out_specs=(spec, spec), check_vma=False
    )
```

```python
import functools

import jax
import jax.numpy as jnp
import numpy as np
from jax import lax
from jax.experimental import pallas as pl
from jax.experimental.pallas import tpu as pltpu
from jax.sharding import PartitionSpec as P

HUBS = ((7, 5, 0), (8, 6, 0), (9, 6, 1), (10, 12, 1), (11, 12, 0))
TRACKS = 2
MESH = pl.DeviceIdType.MESH
HIGHEST = lax.Precision.HIGHEST
F32 = jnp.float32
BETA = 1.0 / 36.0


def line_modes(courant):
    a, b = 4.0 / 9.0, BETA
    near, far = courant * 20.0 / 27.0, courant * 25.0 / 216.0
    top = np.array([b, a, 1.0, a, b])
    bottom = np.array([b + far, a + near, 1.0, a - near, b - far])
    roots = np.real(np.roots(bottom))
    for _ in range(4):
        roots = roots - np.polyval(bottom, roots) / np.polyval(np.polyder(bottom), roots)
    residues = np.polyval(top, roots) / np.polyval(np.polyder(bottom), roots)
    inside = sorted((k for k in range(4) if abs(roots[k]) < 1), key=lambda k: -abs(roots[k]))
    outside = sorted((k for k in range(4) if abs(roots[k]) > 1), key=lambda k: abs(roots[k]))
    forward = [(roots[k], residues[k]) for k in inside]
    backward = [(1.0 / roots[k], residues[k]) for k in outside]
    return top[0] / bottom[0], forward, backward


def tables(n, courant):
    constant, forward, backward = line_modes(courant)
    lag = np.arange(n)[:, None] - np.arange(n)[None, :]
    local = np.zeros((n, n))
    for w, r in forward:
        local += np.where(lag >= 1, r * np.power(w, np.maximum(lag - 1, 0)), 0.0)
    for v, r in backward:
        local -= np.where(lag <= 0, r * np.power(v, np.maximum(1 - lag, 0)), 0.0)
    local += constant * np.eye(n)
    i = np.arange(n)
    (w1, r1), (w3, r3) = forward
    (v2, r2), (v4, r4) = backward
    source = np.stack([r1 * w1 ** (n - 1 - i), -r2 * v2 ** (i + 2), r3 * w3 ** (n - 1 - i), -r4 * v4 ** (i + 2)])
    response = np.stack([w1**i, v2 ** (n - 1 - i), w3**i, v4 ** (n - 1 - i)])
    return local, source, response, w1**n, v2**n


def tiny_off(array):
    out = np.asarray(array, np.float32)
    return np.where(np.abs(out) < np.finfo(np.float32).tiny, np.float32(0), out)


def wait_bytes(ref, sem):
    pltpu.make_async_copy(ref, ref, sem).wait()


def exchange_kernel(q1, q2, nz, ny, planes, n,
                    fields, inv_x, inv_y, consts,
                    x_out, y_out,
                    f, cst, ixv, iyv, pre_y, coef, wx, back, sx, px, pbuf, rb, gsp, gbuf, gpar, fast, sy, yb, yn,
                    load_sem, pair_s, pair_r, fast_s, fast_r, far_s, far_r, give_s, give_r, ret_s, ret_r,
                    ys_s, ys_r, yn_s, yn_r, ready_y, level, relay_y):
    gx, gy = lax.axis_index("gx"), lax.axis_index("gy")
    c, z = lax.rem(gx, 2), lax.div(gx, 2)
    half, quarter = planes // 2, nz // 4
    ahead, behind = z < quarter, z >= quarter

    def at(chips):
        found = z == chips[0]
        for chip_z in chips[1:]:
            found = found | (z == chip_z)
        return found

    spoke = at([z_of for z_of, _, _ in HUBS])
    plain = jnp.logical_not(spoke)
    chunks = 4
    step = planes // chunks
    loads = [pltpu.make_async_copy(consts.at[pl.ds(0, n)], cst.at[pl.ds(0, n)], load_sem.at[chunks])]
    for k in range(chunks):
        loads.append(pltpu.make_async_copy(fields.at[pl.ds(k * step, step)], f.at[pl.ds(k * step, step)], load_sem.at[k]))
    loads.append(pltpu.make_async_copy(inv_x, ixv, load_sem.at[chunks + 1]))
    loads.append(pltpu.make_async_copy(inv_y, iyv, load_sem.at[chunks + 2]))
    rest_rows = pl.ds(n, cst.shape[0] - n)
    loads.append(pltpu.make_async_copy(consts.at[rest_rows], cst.at[rest_rows], load_sem.at[chunks + 3]))
    for load in loads:
        load.start()

    def chip(m):
        return (lax.rem(gx + 2 * m, 2 * nz), gy)

    def along_y(m):
        return (gx, lax.rem(gy + m, ny))

    def spoke_of(k):
        other = 0
        for z_of, z_hub, k_of in HUBS:
            if k_of == k:
                other = jnp.where(z == z_hub, z_of, other)
        return other

    def signal(sem, device):
        pl.semaphore_signal(sem, inc=1, device_id=device, device_id_type=MESH)

    partner = (gx + 1 - 2 * c, gy)
    beside = (lax.rem(gx + 2 * nz - 1 + 2 * c, 2 * nz), gy)

    hub = track = 0
    for z_of, z_hub, k in HUBS:
        hub, track = jnp.where(z == z_of, z_hub, hub), jnp.where(z == z_of, k, track)
    barrier = pltpu.get_barrier_semaphore()
    signal(barrier, partner)
    signal(barrier, beside)

    @pl.when(ahead)
    def _():
        for m in range(1, nz):
            signal(barrier, chip(m))

    for k in range(TRACKS):
        @pl.when(at([z_hub for _, z_hub, k_of in HUBS if k_of == k]))
        def _():
            signal(barrier, (2 * spoke_of(k) + c, gy))

    @pl.when(plain)
    def _():
        for m in range(1, ny):
            signal(barrier, along_y(m))

    def x_sources():
        loads[0].wait()
        for k in range(4):
            wx[k] = jnp.broadcast_to(cst[pl.ds(0, n), pl.ds(4 + k, 1)], (n, n))
        w1, w2, w3, w4 = wx.at[0], wx.at[1], wx.at[2, pl.ds(n // 2, n // 2)], wx.at[3, pl.ds(0, n // 2)]

        def total(v):
            return jnp.sum(jnp.sum(v.reshape(-1, 8, n), axis=0), axis=0, keepdims=True)

        for fz in range(planes):
            if fz % step == 0:
                loads[1 + fz // step].wait()
            cells = f[fz]
            h, p = fz // half, fz % half
            sx[0, h, p:p + 1] = total(cells * w1[...])
            sx[1, h, p:p + 1] = total(cells * w2[...])
            sx[2, h, p:p + 1] = total(cells[n // 2:] * w3[...])
            sx[3, h, p:p + 1] = total(cells[:n // 2] * w4[...])

    def y_sources():
        row32 = lax.broadcasted_iota(jnp.int32, (32, n), 0)
        loads[chunks + 3].wait()
        wsrc = cst[pl.ds(2 * n, 32)]
        for h in range(2):
            acc = jnp.zeros((32, n), F32)
            for p in range(half):
                w = jnp.where(lax.rem(row32, half) == p, wsrc, 0.0)
                acc = acc + lax.dot_general(w, f[h * half + p], (((1,), (1,)), ((), ())),
                                            preferred_element_type=F32, precision=HIGHEST)
            for k in range(4):
                sy[k, h] = acc[k * half:(k + 1) * half]

    def local_products():
        loads[chunks + 1].wait()
        loads[chunks + 2].wait()
        ix = jnp.transpose(jnp.broadcast_to(ixv[...], (n, n)))
        iy = iyv[...]
        for k in range(4):
            coef[k] = cst[pl.ds(0, n), pl.ds(k, 1)] * ix
        coef[4] = ix
        local = cst[pl.ds(n, n)]
        answer = cst[pl.ds(2 * n + 32, 4 * planes)] * iy
        top = answer.astype(jnp.bfloat16).astype(F32)
        rest = answer - top
        row = lax.rem(lax.broadcasted_iota(jnp.int32, (4 * planes, n), 0), planes)

        def plane(fz, carry):
            cells = f[fz]
            x_line = jnp.dot(local, cells, preferred_element_type=F32, precision=HIGHEST)
            x_out[fz] = (cells - x_line) * coef[4]
            y_line = lax.dot_general(cells, local, (((1,), (1,)), ((), ())),
                                     preferred_element_type=F32, precision=HIGHEST)
            pre_y[fz] = (cells - y_line) * iy
            one = jnp.where(row == fz, top, 0.0).astype(jnp.bfloat16)
            two = jnp.where(row == fz, rest, 0.0).astype(jnp.bfloat16)
            back[fz] = jnp.concatenate([one, two, one, two], axis=0)
            return carry

        lax.fori_loop(0, planes, plane, 0, unroll=4)

    def far_send(zd):
        pltpu.make_async_remote_copy(
            pbuf, rb.at[lax.rem(zd - z + nz, nz)], far_s, far_r,
            device_id=(2 * zd + c, gy), device_id_type=MESH).start()

    def y_sends():
        for m in range(1, ny):
            pltpu.make_async_remote_copy(
                sy.at[pl.ds(0, 2)], yb.at[m], ys_s, ys_r, device_id=along_y(m), device_id_type=MESH).start()
        for copy in beyond:
            copy.start()

    beyond = [
        pltpu.make_async_remote_copy(
            sy.at[2 + k], yn.at[k], yn_s.at[k], yn_r.at[k], device_id=along_y(m), device_id_type=MESH)
        for k, m in ((0, 1), (1, ny - 1))
    ]

    pair = pltpu.make_async_remote_copy(sx, px, pair_s, pair_r, device_id=partner, device_id_type=MESH)
    side = pltpu.make_async_remote_copy(sx.at[3 - c], fast, fast_s, fast_r, device_id=beside, device_id_type=MESH)

    counted = jnp.where(ahead, quarter - 1, quarter) + 2

    @pl.when(spoke)
    def _():
        pl.semaphore_wait(barrier, counted + 1)
        signal(ready_y.at[track], (2 * hub + c, gy))

    x_sources()

    @pl.when(plain)
    def _():
        y_sources()

        @pl.when(ahead)
        def _():
            local_products()

        pl.semaphore_wait(barrier, counted + ny - 1)

    pair.start()
    side.start()
    first = c == 0
    pair.wait_recv()
    pbuf[0] = jnp.where(first, q1, 1.0) * sx[0, c] + jnp.where(first, 1.0, q1) * px[0, c]
    pbuf[1] = jnp.where(first, 1.0, q2) * sx[1, c] + jnp.where(first, q2, 1.0) * px[1, c]
    for zd in range(quarter):
        @pl.when(z != zd)
        def _():
            far_send(zd)

    @pl.when(plain)
    def _():
        y_sends()

    for k in range(TRACKS):
        @pl.when(at([z_hub for _, z_hub, k_of in HUBS if k_of == k]))
        def _():
            pl.semaphore_wait(ready_y.at[k], 1)
            for m in range(1, ny):
                signal(level.at[k], along_y(m))

    for k in range(TRACKS):
        @pl.when(at([z_hub for _, z_hub, k_of in HUBS if k_of == k]))
        def _():
            pl.semaphore_wait(level.at[k], ny - 1)
            signal(relay_y, (2 * spoke_of(k) + c, gy))

    @pl.when(spoke)
    def _():
        y_sources()

    @pl.when(behind)
    def _():
        local_products()

    @pl.when(spoke)
    def _():
        pl.semaphore_wait(relay_y, 1)
        y_sends()

    wait_bytes(yb.at[pl.ds(1, ny - 1)], ys_r)
    close1, close2 = 1.0 / (1.0 - q1**ny), 1.0 / (1.0 - q2**ny)
    fy1 = (close1 * q1 ** (ny - 1)) * sy[0]
    fy2 = (close2 * q2 ** (ny - 1)) * sy[1]
    for m in range(1, ny):
        fy1 = fy1 + (close1 * q1 ** (m - 1)) * yb[m, 0]
        fy2 = fy2 + (close2 * q2 ** (ny - m - 1)) * yb[m, 1]
    beyond[0].wait_recv()
    beyond[1].wait_recv()
    fy = jnp.concatenate([v.reshape(planes, n) for v in (fy1, fy2, yn[0], yn[1])], axis=0)
    top = fy.astype(jnp.bfloat16).astype(F32)
    rest = fy - top
    lhs = jnp.concatenate([jnp.transpose(jnp.concatenate([v, v], axis=0)) for v in (top, rest)], axis=1).astype(jnp.bfloat16)
    for fz in range(planes):
        y_out[fz] = pre_y[fz] - jnp.dot(lhs, back[fz], preferred_element_type=F32)

    e1, e2 = q1 * q1, q2 * q2
    close1, close2 = 1.0 / (1.0 - e1**nz), 1.0 / (1.0 - e2**nz)
    turns = nz // quarter

    def incoming(k, to):
        g1 = g2 = None
        for m in range(nz):
            shift = m + k * quarter
            v1, v2 = (pbuf[0], pbuf[1]) if m == 0 else (rb[m, 0], rb[m, 1])
            t1 = (close1 * e1 ** ((shift - 1) % nz)) * v1
            t2 = (close2 * e2 ** ((-shift - 1) % nz)) * v2
            g1, g2 = (t1, t2) if m == 0 else (g1 + t1, g2 + t2)
        to[0] = g1
        to[1] = g2

    ret = pltpu.make_async_remote_copy(gbuf, gpar, ret_s, ret_r, device_id=partner, device_id_type=MESH)

    def give(k):
        return pltpu.make_async_remote_copy(gsp.at[k - 1], gbuf, give_s, give_r,
                                            device_id=chip(k * quarter), device_id_type=MESH)

    @pl.when(ahead)
    def _():
        wait_bytes(rb.at[pl.ds(1, nz - 1)], far_r)
        incoming(0, gbuf)
        ret.start()
        for k in range(1, turns):
            incoming(k, gsp.at[k - 1])
            give(k).start()

    @pl.when(behind)
    def _():
        wait_bytes(gbuf, give_r)
        ret.start()

    side.wait_recv()
    a1 = jnp.where(first, 1.0, q1)
    b1 = jnp.where(first, 0.0, 1.0)
    a2 = jnp.where(first, q2, 1.0)
    b2 = jnp.where(first, 1.0, 0.0)
    f3 = jnp.where(first, fast[...], px[2])
    f4 = jnp.where(first, px[3], fast[...])
    pair.wait_send()
    side.wait_send()
    beyond[0].wait_send()
    beyond[1].wait_send()

    @pl.when(ahead)
    def _():
        wait_bytes(rb.at[pl.ds(0, quarter - 1)], far_s)

    @pl.when(behind)
    def _():
        wait_bytes(rb.at[pl.ds(0, quarter)], far_s)

    wait_bytes(yb.at[pl.ds(1, ny - 1)], ys_s)
    ret.wait_recv()
    own1, own2, par1, par2 = gbuf[0], gbuf[1], gpar[0], gpar[1]
    for h in range(2):
        mine = c == h
        f1 = a1 * jnp.where(mine, own1, par1) + b1 * px[0, h]
        f2 = a2 * jnp.where(mine, own2, par2) + b2 * px[1, h]
        for p in range(half):
            fz = h * half + p
            fix = coef[0] * f1[p:p + 1] + coef[1] * f2[p:p + 1]
            x_out[fz] = x_out[fz] - fix - coef[2] * f3[h, p:p + 1] - coef[3] * f4[h, p:p + 1]
    ret.wait_send()

    @pl.when(ahead)
    def _():
        wait_bytes(gsp, give_s)


def store_kernel(x_in, y_in, x_out, y_out, sem):
    parts = 4
    rows = x_in.shape[0] // parts
    copies = []
    for k in range(parts):
        part = pl.ds(k * rows, rows)
        copies.append(pltpu.make_async_copy(x_in.at[part], x_out.at[part], sem.at[2 * k]))
        copies.append(pltpu.make_async_copy(y_in.at[part], y_out.at[part], sem.at[2 * k + 1]))
    for copy in copies:
        copy.start()
    for copy in copies:
        copy.wait()


def on_device(fields, inv_dx, inv_dy):
    nfield, nplane, n, ncol = fields.shape
    gxn, gyn = lax.axis_size("gx"), lax.axis_size("gy")
    planes, nz = nfield * nplane, gxn // 2
    courant = float(n * gxn // 16)
    local, source, response, q1, q2 = tables(n, courant)
    half = planes // 2
    consts = np.concatenate([
        np.pad(np.concatenate([response, source]).T, ((0, 0), (0, n - 8))),
        local,
        np.repeat(source, half, axis=0),
        np.repeat(response, planes, axis=0),
    ], axis=0)
    consts = jnp.asarray(tiny_off(consts))
    block = jax.ShapeDtypeStruct((planes, n, n), F32)
    hbm = pl.BlockSpec(memory_space=pltpu.HBM)
    vmem = pl.BlockSpec(memory_space=pltpu.VMEM)
    vm = lambda *shape: pltpu.VMEM(shape, F32)
    dma = pltpu.SemaphoreType.DMA
    x_pre, y_pre = pl.pallas_call(
        functools.partial(exchange_kernel, float(q1), float(q2), nz, gyn, planes, n),
        out_shape=(pltpu.VMEM((planes, n, n), F32), pltpu.VMEM((planes, n, n), F32)),
        in_specs=[hbm] * 4,
        out_specs=(vmem, vmem),
        scratch_shapes=[
            vm(planes, n, n), vm(*consts.shape), vm(1, n), vm(1, n), vm(planes, n, n), vm(5, n, n), vm(4, n, n),
            pltpu.VMEM((planes, 16 * planes, n), jnp.bfloat16),
            vm(4, 2, half, n), vm(4, 2, half, n), vm(2, half, n), vm(nz, 2, half, n), vm(3, 2, half, n), vm(2, half, n), vm(2, half, n),
            vm(2, half, n), vm(4, 2, half, n), vm(gyn, 2, 2, half, n), vm(2, 2, half, n),
            dma((8,)), dma, dma, dma, dma, dma, dma, dma, dma, dma, dma, dma, dma, dma((2,)), dma((2,)),
            pltpu.SemaphoreType.REGULAR((TRACKS,)), pltpu.SemaphoreType.REGULAR((TRACKS,)), pltpu.SemaphoreType.REGULAR,
        ],
        compiler_params=pltpu.CompilerParams(
            collective_id=0, has_side_effects=True, vmem_limit_bytes=24 * 1024 * 1024),
        name="exchange",
    )(*(pltpu.with_memory_space_constraint(a, pltpu.HBM)
        for a in (fields.reshape(planes, n, n), inv_dx.reshape(1, n), inv_dy.reshape(1, n), consts)))
    x_derivs, y_derivs = pl.pallas_call(
        store_kernel,
        out_shape=(block, block),
        in_specs=[vmem, vmem],
        out_specs=(hbm, hbm),
        scratch_shapes=[dma((8,))],
        compiler_params=pltpu.CompilerParams(vmem_limit_bytes=24 * 1024 * 1024),
        name="store",
    )(x_pre, y_pre)
    return x_derivs.reshape(fields.shape), y_derivs.reshape(fields.shape)


def solution(mesh):
    spec = P(None, None, "gx", "gy")
    return jax.shard_map(
        on_device, mesh=mesh, in_specs=(spec, P("gx"), P("gy")), out_specs=(spec, spec), check_vma=False
    )
```

```python
import functools

import jax
import jax.numpy as jnp
import numpy as np
from jax import lax
from jax.experimental import pallas as pl
from jax.experimental.pallas import tpu as pltpu
from jax.sharding import PartitionSpec as P

HUBS = ((7, 5, 0), (8, 6, 0), (9, 6, 1), (10, 13, 2), (11, 13, 1), (12, 13, 0))
TRACKS = 3
MESH = pl.DeviceIdType.MESH
HIGHEST = lax.Precision.HIGHEST
F32 = jnp.float32
BETA = 1.0 / 36.0


def line_modes(courant):
    a, b = 4.0 / 9.0, BETA
    near, far = courant * 20.0 / 27.0, courant * 25.0 / 216.0
    top = np.array([b, a, 1.0, a, b])
    bottom = np.array([b + far, a + near, 1.0, a - near, b - far])
    roots = np.real(np.roots(bottom))
    for _ in range(4):
        roots = roots - np.polyval(bottom, roots) / np.polyval(np.polyder(bottom), roots)
    residues = np.polyval(top, roots) / np.polyval(np.polyder(bottom), roots)
    inside = sorted((k for k in range(4) if abs(roots[k]) < 1), key=lambda k: -abs(roots[k]))
    outside = sorted((k for k in range(4) if abs(roots[k]) > 1), key=lambda k: abs(roots[k]))
    forward = [(roots[k], residues[k]) for k in inside]
    backward = [(1.0 / roots[k], residues[k]) for k in outside]
    return top[0] / bottom[0], forward, backward


def tables(n, courant):
    constant, forward, backward = line_modes(courant)
    lag = np.arange(n)[:, None] - np.arange(n)[None, :]
    local = np.zeros((n, n))
    for w, r in forward:
        local += np.where(lag >= 1, r * np.power(w, np.maximum(lag - 1, 0)), 0.0)
    for v, r in backward:
        local -= np.where(lag <= 0, r * np.power(v, np.maximum(1 - lag, 0)), 0.0)
    local += constant * np.eye(n)
    i = np.arange(n)
    (w1, r1), (w3, r3) = forward
    (v2, r2), (v4, r4) = backward
    source = np.stack([r1 * w1 ** (n - 1 - i), -r2 * v2 ** (i + 2), r3 * w3 ** (n - 1 - i), -r4 * v4 ** (i + 2)])
    response = np.stack([w1**i, v2 ** (n - 1 - i), w3**i, v4 ** (n - 1 - i)])
    return local, source, response, w1**n, v2**n


def tiny_off(array):
    out = np.asarray(array, np.float32)
    return np.where(np.abs(out) < np.finfo(np.float32).tiny, np.float32(0), out)


def wait_bytes(ref, sem):
    pltpu.make_async_copy(ref, ref, sem).wait()


def exchange_kernel(q1, q2, nz, ny, planes, n,
                    fields, inv_x, inv_y, consts,
                    x_out, y_out,
                    f, cst, ixv, iyv, pre_y, coef, wx, back, sx, px, pbuf, rb, gsp, gbuf, gpar, fast, sy, yb, yn,
                    load_sem, pair_s, pair_r, fast_s, fast_r, far_s, far_r, give_s, give_r, ret_s, ret_r,
                    ys_s, ys_r, yn_s, yn_r, ready_y, level, relay_y):
    gx, gy = lax.axis_index("gx"), lax.axis_index("gy")
    c, z = lax.rem(gx, 2), lax.div(gx, 2)
    half, quarter = planes // 2, nz // 4
    ahead, behind = z < quarter, z >= quarter

    def at(chips):
        found = z == chips[0]
        for chip_z in chips[1:]:
            found = found | (z == chip_z)
        return found

    spoke = at([z_of for z_of, _, _ in HUBS])
    plain = jnp.logical_not(spoke)
    chunks = 4
    step = planes // chunks
    loads = [pltpu.make_async_copy(consts.at[pl.ds(0, n)], cst.at[pl.ds(0, n)], load_sem.at[chunks])]
    for k in range(chunks):
        loads.append(pltpu.make_async_copy(fields.at[pl.ds(k * step, step)], f.at[pl.ds(k * step, step)], load_sem.at[k]))
    loads.append(pltpu.make_async_copy(inv_x, ixv, load_sem.at[chunks + 1]))
    loads.append(pltpu.make_async_copy(inv_y, iyv, load_sem.at[chunks + 2]))
    rest_rows = pl.ds(n, cst.shape[0] - n)
    loads.append(pltpu.make_async_copy(consts.at[rest_rows], cst.at[rest_rows], load_sem.at[chunks + 3]))
    for load in loads:
        load.start()

    def chip(m):
        return (lax.rem(gx + 2 * m, 2 * nz), gy)

    def along_y(m):
        return (gx, lax.rem(gy + m, ny))

    def spoke_of(k):
        other = 0
        for z_of, z_hub, k_of in HUBS:
            if k_of == k:
                other = jnp.where(z == z_hub, z_of, other)
        return other

    def signal(sem, device):
        pl.semaphore_signal(sem, inc=1, device_id=device, device_id_type=MESH)

    partner = (gx + 1 - 2 * c, gy)
    beside = (lax.rem(gx + 2 * nz - 1 + 2 * c, 2 * nz), gy)

    hub = track = 0
    for z_of, z_hub, k in HUBS:
        hub, track = jnp.where(z == z_of, z_hub, hub), jnp.where(z == z_of, k, track)
    barrier = pltpu.get_barrier_semaphore()
    signal(barrier, partner)
    signal(barrier, beside)

    @pl.when(ahead)
    def _():
        for m in range(1, nz):
            signal(barrier, chip(m))

    for k in range(TRACKS):
        @pl.when(at([z_hub for _, z_hub, k_of in HUBS if k_of == k]))
        def _():
            signal(barrier, (2 * spoke_of(k) + c, gy))

    @pl.when(plain)
    def _():
        for m in range(1, ny):
            signal(barrier, along_y(m))

    def x_sources():
        loads[0].wait()
        for k in range(4):
            wx[k] = jnp.broadcast_to(cst[pl.ds(0, n), pl.ds(4 + k, 1)], (n, n))
        w1, w2, w3, w4 = wx.at[0], wx.at[1], wx.at[2, pl.ds(n // 2, n // 2)], wx.at[3, pl.ds(0, n // 2)]

        def total(v):
            return jnp.sum(jnp.sum(v.reshape(-1, 8, n), axis=0), axis=0, keepdims=True)

        for fz in range(planes):
            if fz % step == 0:
                loads[1 + fz // step].wait()
            cells = f[fz]
            h, p = fz // half, fz % half
            sx[0, h, p:p + 1] = total(cells * w1[...])
            sx[1, h, p:p + 1] = total(cells * w2[...])
            sx[2, h, p:p + 1] = total(cells[n // 2:] * w3[...])
            sx[3, h, p:p + 1] = total(cells[:n // 2] * w4[...])

    def y_sources():
        row32 = lax.broadcasted_iota(jnp.int32, (32, n), 0)
        loads[chunks + 3].wait()
        wsrc = cst[pl.ds(2 * n, 32)]
        for h in range(2):
            acc = jnp.zeros((32, n), F32)
            for p in range(half):
                w = jnp.where(lax.rem(row32, half) == p, wsrc, 0.0)
                acc = acc + lax.dot_general(w, f[h * half + p], (((1,), (1,)), ((), ())),
                                            preferred_element_type=F32, precision=HIGHEST)
            for k in range(4):
                sy[k, h] = acc[k * half:(k + 1) * half]

    def local_products():
        loads[chunks + 1].wait()
        loads[chunks + 2].wait()
        ix = jnp.transpose(jnp.broadcast_to(ixv[...], (n, n)))
        iy = iyv[...]
        for k in range(4):
            coef[k] = cst[pl.ds(0, n), pl.ds(k, 1)] * ix
        coef[4] = ix
        local = cst[pl.ds(n, n)]
        answer = cst[pl.ds(2 * n + 32, 4 * planes)] * iy
        top = answer.astype(jnp.bfloat16).astype(F32)
        rest = answer - top
        row = lax.rem(lax.broadcasted_iota(jnp.int32, (4 * planes, n), 0), planes)

        def plane(fz, carry):
            cells = f[fz]
            x_line = jnp.dot(local, cells, preferred_element_type=F32, precision=HIGHEST)
            x_out[fz] = (cells - x_line) * coef[4]
            y_line = lax.dot_general(cells, local, (((1,), (1,)), ((), ())),
                                     preferred_element_type=F32, precision=HIGHEST)
            pre_y[fz] = (cells - y_line) * iy
            one = jnp.where(row == fz, top, 0.0).astype(jnp.bfloat16)
            two = jnp.where(row == fz, rest, 0.0).astype(jnp.bfloat16)
            back[fz] = jnp.concatenate([one, two, one, two], axis=0)
            return carry

        lax.fori_loop(0, planes, plane, 0, unroll=4)

    def far_send(zd):
        pltpu.make_async_remote_copy(
            pbuf, rb.at[lax.rem(zd - z + nz, nz)], far_s, far_r,
            device_id=(2 * zd + c, gy), device_id_type=MESH).start()

    def y_sends():
        for m in range(1, ny):
            pltpu.make_async_remote_copy(
                sy.at[pl.ds(0, 2)], yb.at[m], ys_s, ys_r, device_id=along_y(m), device_id_type=MESH).start()
        for copy in beyond:
            copy.start()

    beyond = [
        pltpu.make_async_remote_copy(
            sy.at[2 + k], yn.at[k], yn_s.at[k], yn_r.at[k], device_id=along_y(m), device_id_type=MESH)
        for k, m in ((0, 1), (1, ny - 1))
    ]

    pair = pltpu.make_async_remote_copy(sx, px, pair_s, pair_r, device_id=partner, device_id_type=MESH)
    side = pltpu.make_async_remote_copy(sx.at[3 - c], fast, fast_s, fast_r, device_id=beside, device_id_type=MESH)

    counted = jnp.where(ahead, quarter - 1, quarter) + 2

    x_sources()

    @pl.when(spoke)
    def _():
        pl.semaphore_wait(barrier, counted + 1)
        signal(ready_y.at[track], (2 * hub + c, gy))

    @pl.when(plain)
    def _():
        y_sources()

        @pl.when(ahead)
        def _():
            local_products()

        pl.semaphore_wait(barrier, counted + ny - 1)

    def hear_spokes(among):
        for k in range(TRACKS):
            hubs = [z_hub for _, z_hub, k_of in HUBS if k_of == k and among(z_hub)]
            if hubs:
                @pl.when(at(hubs))
                def _():
                    pl.semaphore_wait(ready_y.at[k], 1)
                    for m in range(1, ny):
                        signal(level.at[k], along_y(m))

    pair.start()
    side.start()
    hear_spokes(lambda z_hub: z_hub >= nz // 2)
    first = c == 0
    pair.wait_recv()
    pbuf[0] = jnp.where(first, q1, 1.0) * sx[0, c] + jnp.where(first, 1.0, q1) * px[0, c]
    pbuf[1] = jnp.where(first, 1.0, q2) * sx[1, c] + jnp.where(first, q2, 1.0) * px[1, c]
    for zd in range(quarter):
        @pl.when(z != zd)
        def _():
            far_send(zd)

    @pl.when(plain)
    def _():
        y_sends()

    hear_spokes(lambda z_hub: z_hub < nz // 2)

    for k in range(TRACKS):
        @pl.when(at([z_hub for _, z_hub, k_of in HUBS if k_of == k]))
        def _():
            pl.semaphore_wait(level.at[k], ny - 1)
            signal(relay_y, (2 * spoke_of(k) + c, gy))

    @pl.when(spoke)
    def _():
        y_sources()

    @pl.when(behind)
    def _():
        local_products()

    @pl.when(spoke)
    def _():
        pl.semaphore_wait(relay_y, 1)
        y_sends()

    wait_bytes(yb.at[pl.ds(1, ny - 1)], ys_r)
    close1, close2 = 1.0 / (1.0 - q1**ny), 1.0 / (1.0 - q2**ny)
    fy1 = (close1 * q1 ** (ny - 1)) * sy[0]
    fy2 = (close2 * q2 ** (ny - 1)) * sy[1]
    for m in range(1, ny):
        fy1 = fy1 + (close1 * q1 ** (m - 1)) * yb[m, 0]
        fy2 = fy2 + (close2 * q2 ** (ny - m - 1)) * yb[m, 1]
    beyond[0].wait_recv()
    beyond[1].wait_recv()
    fy = jnp.concatenate([v.reshape(planes, n) for v in (fy1, fy2, yn[0], yn[1])], axis=0)
    top = fy.astype(jnp.bfloat16).astype(F32)
    rest = fy - top
    lhs = jnp.concatenate([jnp.transpose(jnp.concatenate([v, v], axis=0)) for v in (top, rest)], axis=1).astype(jnp.bfloat16)
    for fz in range(planes):
        y_out[fz] = pre_y[fz] - jnp.dot(lhs, back[fz], preferred_element_type=F32)

    e1, e2 = q1 * q1, q2 * q2
    close1, close2 = 1.0 / (1.0 - e1**nz), 1.0 / (1.0 - e2**nz)
    turns = nz // quarter

    def incoming(k, to):
        g1 = g2 = None
        for m in range(nz):
            shift = m + k * quarter
            v1, v2 = (pbuf[0], pbuf[1]) if m == 0 else (rb[m, 0], rb[m, 1])
            t1 = (close1 * e1 ** ((shift - 1) % nz)) * v1
            t2 = (close2 * e2 ** ((-shift - 1) % nz)) * v2
            g1, g2 = (t1, t2) if m == 0 else (g1 + t1, g2 + t2)
        to[0] = g1
        to[1] = g2

    ret = pltpu.make_async_remote_copy(gbuf, gpar, ret_s, ret_r, device_id=partner, device_id_type=MESH)

    def give(k):
        return pltpu.make_async_remote_copy(gsp.at[k - 1], gbuf, give_s, give_r,
                                            device_id=chip(k * quarter), device_id_type=MESH)

    @pl.when(ahead)
    def _():
        wait_bytes(rb.at[pl.ds(1, nz - 1)], far_r)
        incoming(0, gbuf)
        ret.start()
        for k in sorted(range(1, turns), key=lambda k: -min(k, turns - k)):
            incoming(k, gsp.at[k - 1])
            give(k).start()

    @pl.when(behind)
    def _():
        wait_bytes(gbuf, give_r)
        ret.start()

    side.wait_recv()
    a1 = jnp.where(first, 1.0, q1)
    b1 = jnp.where(first, 0.0, 1.0)
    a2 = jnp.where(first, q2, 1.0)
    b2 = jnp.where(first, 1.0, 0.0)
    f3 = jnp.where(first, fast[...], px[2])
    f4 = jnp.where(first, px[3], fast[...])
    pair.wait_send()
    side.wait_send()
    beyond[0].wait_send()
    beyond[1].wait_send()

    @pl.when(ahead)
    def _():
        wait_bytes(rb.at[pl.ds(0, quarter - 1)], far_s)

    @pl.when(behind)
    def _():
        wait_bytes(rb.at[pl.ds(0, quarter)], far_s)

    wait_bytes(yb.at[pl.ds(1, ny - 1)], ys_s)
    ret.wait_recv()
    own1, own2, par1, par2 = gbuf[0], gbuf[1], gpar[0], gpar[1]
    for h in range(2):
        mine = c == h
        f1 = a1 * jnp.where(mine, own1, par1) + b1 * px[0, h]
        f2 = a2 * jnp.where(mine, own2, par2) + b2 * px[1, h]
        for p in range(half):
            fz = h * half + p
            fix = coef[0] * f1[p:p + 1] + coef[1] * f2[p:p + 1]
            x_out[fz] = x_out[fz] - fix - coef[2] * f3[h, p:p + 1] - coef[3] * f4[h, p:p + 1]
    ret.wait_send()

    @pl.when(ahead)
    def _():
        wait_bytes(gsp, give_s)


def store_kernel(x_in, y_in, x_out, y_out, sem):
    parts = 4
    rows = x_in.shape[0] // parts
    copies = []
    for k in range(parts):
        part = pl.ds(k * rows, rows)
        copies.append(pltpu.make_async_copy(x_in.at[part], x_out.at[part], sem.at[2 * k]))
        copies.append(pltpu.make_async_copy(y_in.at[part], y_out.at[part], sem.at[2 * k + 1]))
    for copy in copies:
        copy.start()
    for copy in copies:
        copy.wait()


def on_device(fields, inv_dx, inv_dy):
    nfield, nplane, n, ncol = fields.shape
    gxn, gyn = lax.axis_size("gx"), lax.axis_size("gy")
    planes, nz = nfield * nplane, gxn // 2
    courant = float(n * gxn // 16)
    local, source, response, q1, q2 = tables(n, courant)
    half = planes // 2
    consts = np.concatenate([
        np.pad(np.concatenate([response, source]).T, ((0, 0), (0, n - 8))),
        local,
        np.repeat(source, half, axis=0),
        np.repeat(response, planes, axis=0),
    ], axis=0)
    consts = jnp.asarray(tiny_off(consts))
    block = jax.ShapeDtypeStruct((planes, n, n), F32)
    hbm = pl.BlockSpec(memory_space=pltpu.HBM)
    vmem = pl.BlockSpec(memory_space=pltpu.VMEM)
    vm = lambda *shape: pltpu.VMEM(shape, F32)
    dma = pltpu.SemaphoreType.DMA
    x_pre, y_pre = pl.pallas_call(
        functools.partial(exchange_kernel, float(q1), float(q2), nz, gyn, planes, n),
        out_shape=(pltpu.VMEM((planes, n, n), F32), pltpu.VMEM((planes, n, n), F32)),
        in_specs=[hbm] * 4,
        out_specs=(vmem, vmem),
        scratch_shapes=[
            vm(planes, n, n), vm(*consts.shape), vm(1, n), vm(1, n), vm(planes, n, n), vm(5, n, n), vm(4, n, n),
            pltpu.VMEM((planes, 16 * planes, n), jnp.bfloat16),
            vm(4, 2, half, n), vm(4, 2, half, n), vm(2, half, n), vm(nz, 2, half, n), vm(3, 2, half, n), vm(2, half, n), vm(2, half, n),
            vm(2, half, n), vm(4, 2, half, n), vm(gyn, 2, 2, half, n), vm(2, 2, half, n),
            dma((8,)), dma, dma, dma, dma, dma, dma, dma, dma, dma, dma, dma, dma, dma((2,)), dma((2,)),
            pltpu.SemaphoreType.REGULAR((TRACKS,)), pltpu.SemaphoreType.REGULAR((TRACKS,)), pltpu.SemaphoreType.REGULAR,
        ],
        compiler_params=pltpu.CompilerParams(
            collective_id=0, has_side_effects=True, vmem_limit_bytes=24 * 1024 * 1024),
        name="exchange",
    )(*(pltpu.with_memory_space_constraint(a, pltpu.HBM)
        for a in (fields.reshape(planes, n, n), inv_dx.reshape(1, n), inv_dy.reshape(1, n), consts)))
    x_derivs, y_derivs = pl.pallas_call(
        store_kernel,
        out_shape=(block, block),
        in_specs=[vmem, vmem],
        out_specs=(hbm, hbm),
        scratch_shapes=[dma((8,))],
        compiler_params=pltpu.CompilerParams(vmem_limit_bytes=24 * 1024 * 1024),
        name="store",
    )(x_pre, y_pre)
    return x_derivs.reshape(fields.shape), y_derivs.reshape(fields.shape)


def solution(mesh):
    spec = P(None, None, "gx", "gy")
    return jax.shard_map(
        on_device, mesh=mesh, in_specs=(spec, P("gx"), P("gy")), out_specs=(spec, spec), check_vma=False
    )
```

```python
import functools

import jax
import jax.numpy as jnp
import numpy as np
from jax import lax
from jax.experimental import pallas as pl
from jax.experimental.pallas import tpu as pltpu
from jax.sharding import PartitionSpec as P

HUBS = ((7, 5, 0), (8, 6, 0), (9, 6, 1), (10, 13, 2), (11, 13, 1), (12, 13, 0))
TRACKS = 3
MESH = pl.DeviceIdType.MESH
HIGHEST = lax.Precision.HIGHEST
F32 = jnp.float32
BETA = 1.0 / 36.0


def line_modes(courant):
    a, b = 4.0 / 9.0, BETA
    near, far = courant * 20.0 / 27.0, courant * 25.0 / 216.0
    top = np.array([b, a, 1.0, a, b])
    bottom = np.array([b + far, a + near, 1.0, a - near, b - far])
    roots = np.real(np.roots(bottom))
    for _ in range(4):
        roots = roots - np.polyval(bottom, roots) / np.polyval(np.polyder(bottom), roots)
    residues = np.polyval(top, roots) / np.polyval(np.polyder(bottom), roots)
    inside = sorted((k for k in range(4) if abs(roots[k]) < 1), key=lambda k: -abs(roots[k]))
    outside = sorted((k for k in range(4) if abs(roots[k]) > 1), key=lambda k: abs(roots[k]))
    forward = [(roots[k], residues[k]) for k in inside]
    backward = [(1.0 / roots[k], residues[k]) for k in outside]
    return top[0] / bottom[0], forward, backward


def power(root, exponent):
    size = jnp.exp(exponent.astype(F32) * float(np.log(abs(root))))
    return size if root > 0 else jnp.where(lax.rem(exponent, 2) == 1, -size, size)


def sources(modes, n, i):
    _, ((w1, r1), (w3, r3)), ((v2, r2), (v4, r4)) = modes
    return (float(r1) * power(w1, n - 1 - i), float(-r2) * power(v2, i + 2),
            float(r3) * power(w3, n - 1 - i), float(-r4) * power(v4, i + 2))


def responses(modes, n, i):
    _, ((w1, _), (w3, _)), ((v2, _), (v4, _)) = modes
    return power(w1, i), power(v2, n - 1 - i), power(w3, i), power(v4, n - 1 - i)


def local_table(modes, lag):
    constant, ((w1, r1), (w3, r3)), ((v2, r2), (v4, r4)) = modes
    up, down = jnp.maximum(lag - 1, 0), jnp.maximum(1 - lag, 0)
    above = float(r1) * power(w1, up) + float(r3) * power(w3, up)
    below = float(-r2) * power(v2, down) + float(-r4) * power(v4, down)
    return jnp.where(lag >= 1, above, below) + jnp.where(lag == 0, float(constant), 0.0)


def wait_bytes(ref, sem):
    pltpu.make_async_copy(ref, ref, sem).wait()


def exchange_kernel(modes, q1, q2, nz, ny, planes, n,
                    fields, inv_x, inv_y,
                    x_out, y_out,
                    f, ixv, iyv, pre_y, coef, wx, back, sx, px, pbuf, rb, gsp, gbuf, gpar, fast, sy, yb, yn,
                    load_sem, pair_s, pair_r, fast_s, fast_r, far_s, far_r, give_s, give_r, ret_s, ret_r,
                    ys_s, ys_r, yn_s, yn_r, ready_y, level, relay_y):
    gx, gy = lax.axis_index("gx"), lax.axis_index("gy")
    c, z = lax.rem(gx, 2), lax.div(gx, 2)
    half, quarter = planes // 2, nz // 4
    ahead, behind = z < quarter, z >= quarter

    def at(chips):
        found = z == chips[0]
        for chip_z in chips[1:]:
            found = found | (z == chip_z)
        return found

    spoke = at([z_of for z_of, _, _ in HUBS])
    plain = jnp.logical_not(spoke)
    chunks = 4
    step = planes // chunks
    loads = []
    for k in range(chunks):
        loads.append(pltpu.make_async_copy(fields.at[pl.ds(k * step, step)], f.at[pl.ds(k * step, step)], load_sem.at[k]))
    loads.append(pltpu.make_async_copy(inv_x, ixv, load_sem.at[chunks + 1]))
    loads.append(pltpu.make_async_copy(inv_y, iyv, load_sem.at[chunks + 2]))
    for load in loads:
        load.start()

    def chip(m):
        return (lax.rem(gx + 2 * m, 2 * nz), gy)

    def along_y(m):
        return (gx, lax.rem(gy + m, ny))

    def spoke_of(k):
        other = 0
        for z_of, z_hub, k_of in HUBS:
            if k_of == k:
                other = jnp.where(z == z_hub, z_of, other)
        return other

    def signal(sem, device):
        pl.semaphore_signal(sem, inc=1, device_id=device, device_id_type=MESH)

    partner = (gx + 1 - 2 * c, gy)
    beside = (lax.rem(gx + 2 * nz - 1 + 2 * c, 2 * nz), gy)

    hub = track = 0
    for z_of, z_hub, k in HUBS:
        hub, track = jnp.where(z == z_of, z_hub, hub), jnp.where(z == z_of, k, track)
    barrier = pltpu.get_barrier_semaphore()
    signal(barrier, partner)
    signal(barrier, beside)

    @pl.when(ahead)
    def _():
        for m in range(1, nz):
            signal(barrier, chip(m))

    for k in range(TRACKS):
        @pl.when(at([z_hub for _, z_hub, k_of in HUBS if k_of == k]))
        def _():
            signal(barrier, (2 * spoke_of(k) + c, gy))

    @pl.when(plain)
    def _():
        for m in range(1, ny):
            signal(barrier, along_y(m))

    row, col = (lax.broadcasted_iota(jnp.int32, (n, n), d) for d in (0, 1))

    def x_sources():
        for k, weights in enumerate(sources(modes, n, row)):
            wx[k] = weights
        w1, w2, w3, w4 = wx.at[0], wx.at[1], wx.at[2, pl.ds(n // 2, n // 2)], wx.at[3, pl.ds(0, n // 2)]

        def total(v):
            return jnp.sum(jnp.sum(v.reshape(-1, 8, n), axis=0), axis=0, keepdims=True)

        for fz in range(planes):
            if fz % step == 0:
                loads[fz // step].wait()
            cells = f[fz]
            h, p = fz // half, fz % half
            sx[0, h, p:p + 1] = total(cells * w1[...])
            sx[1, h, p:p + 1] = total(cells * w2[...])
            sx[2, h, p:p + 1] = total(cells[n // 2:] * w3[...])
            sx[3, h, p:p + 1] = total(cells[:n // 2] * w4[...])

    def y_sources():
        row32 = lax.broadcasted_iota(jnp.int32, (32, n), 0)
        wsrc = jnp.concatenate(sources(modes, n, col[:half]), axis=0)
        for h in range(2):
            acc = jnp.zeros((32, n), F32)
            for p in range(half):
                w = jnp.where(lax.rem(row32, half) == p, wsrc, 0.0)
                acc = acc + lax.dot_general(w, f[h * half + p], (((1,), (1,)), ((), ())),
                                            preferred_element_type=F32, precision=HIGHEST)
            for k in range(4):
                sy[k, h] = acc[k * half:(k + 1) * half]

    def local_products():
        loads[chunks].wait()
        loads[chunks + 1].wait()
        ix = jnp.transpose(jnp.broadcast_to(ixv[...], (n, n)))
        iy = iyv[...]
        for k, weights in enumerate(responses(modes, n, row)):
            coef[k] = weights * ix
        coef[4] = ix
        local = local_table(modes, row - col)
        answer = jnp.concatenate(responses(modes, n, col[:planes]), axis=0) * iy
        top = answer.astype(jnp.bfloat16).astype(F32)
        rest = answer - top
        own = lax.rem(lax.broadcasted_iota(jnp.int32, (4 * planes, n), 0), planes)

        def plane(fz, carry):
            cells = f[fz]
            x_line = jnp.dot(local, cells, preferred_element_type=F32, precision=HIGHEST)
            x_out[fz] = (cells - x_line) * coef[4]
            y_line = lax.dot_general(cells, local, (((1,), (1,)), ((), ())),
                                     preferred_element_type=F32, precision=HIGHEST)
            pre_y[fz] = (cells - y_line) * iy
            one = jnp.where(own == fz, top, 0.0).astype(jnp.bfloat16)
            two = jnp.where(own == fz, rest, 0.0).astype(jnp.bfloat16)
            back[fz] = jnp.concatenate([one, two, one, two], axis=0)
            return carry

        lax.fori_loop(0, planes, plane, 0, unroll=4)

    def far_send(zd):
        pltpu.make_async_remote_copy(
            pbuf, rb.at[lax.rem(zd - z + nz, nz)], far_s, far_r,
            device_id=(2 * zd + c, gy), device_id_type=MESH).start()

    def y_sends():
        for m in range(1, ny):
            pltpu.make_async_remote_copy(
                sy.at[pl.ds(0, 2)], yb.at[m], ys_s, ys_r, device_id=along_y(m), device_id_type=MESH).start()
        for copy in beyond:
            copy.start()

    beyond = [
        pltpu.make_async_remote_copy(
            sy.at[2 + k], yn.at[k], yn_s.at[k], yn_r.at[k], device_id=along_y(m), device_id_type=MESH)
        for k, m in ((0, 1), (1, ny - 1))
    ]

    pair = pltpu.make_async_remote_copy(sx, px, pair_s, pair_r, device_id=partner, device_id_type=MESH)
    side = pltpu.make_async_remote_copy(sx.at[3 - c], fast, fast_s, fast_r, device_id=beside, device_id_type=MESH)

    counted = jnp.where(ahead, quarter - 1, quarter) + 2

    x_sources()

    @pl.when(spoke)
    def _():
        pl.semaphore_wait(barrier, counted + 1)
        signal(ready_y.at[track], (2 * hub + c, gy))

    @pl.when(plain)
    def _():
        y_sources()

        @pl.when(ahead)
        def _():
            local_products()

        pl.semaphore_wait(barrier, counted + ny - 1)

    def hear_spokes(among):
        for k in range(TRACKS):
            hubs = [z_hub for _, z_hub, k_of in HUBS if k_of == k and among(z_hub)]
            if hubs:
                @pl.when(at(hubs))
                def _():
                    pl.semaphore_wait(ready_y.at[k], 1)
                    for m in range(1, ny):
                        signal(level.at[k], along_y(m))

    pair.start()
    side.start()
    hear_spokes(lambda z_hub: z_hub >= nz // 2)
    first = c == 0
    pair.wait_recv()
    pbuf[0] = jnp.where(first, q1, 1.0) * sx[0, c] + jnp.where(first, 1.0, q1) * px[0, c]
    pbuf[1] = jnp.where(first, 1.0, q2) * sx[1, c] + jnp.where(first, q2, 1.0) * px[1, c]
    for zd in range(quarter):
        @pl.when(z != zd)
        def _():
            far_send(zd)

    @pl.when(plain)
    def _():
        y_sends()

    hear_spokes(lambda z_hub: z_hub < nz // 2)

    for k in range(TRACKS):
        @pl.when(at([z_hub for _, z_hub, k_of in HUBS if k_of == k]))
        def _():
            pl.semaphore_wait(level.at[k], ny - 1)
            signal(relay_y, (2 * spoke_of(k) + c, gy))

    @pl.when(spoke)
    def _():
        y_sources()

    @pl.when(behind)
    def _():
        local_products()

    @pl.when(spoke)
    def _():
        pl.semaphore_wait(relay_y, 1)
        y_sends()

    wait_bytes(yb.at[pl.ds(1, ny - 1)], ys_r)
    close1, close2 = 1.0 / (1.0 - q1**ny), 1.0 / (1.0 - q2**ny)
    fy1 = (close1 * q1 ** (ny - 1)) * sy[0]
    fy2 = (close2 * q2 ** (ny - 1)) * sy[1]
    for m in range(1, ny):
        fy1 = fy1 + (close1 * q1 ** (m - 1)) * yb[m, 0]
        fy2 = fy2 + (close2 * q2 ** (ny - m - 1)) * yb[m, 1]
    beyond[0].wait_recv()
    beyond[1].wait_recv()
    fy = jnp.concatenate([v.reshape(planes, n) for v in (fy1, fy2, yn[0], yn[1])], axis=0)
    top = fy.astype(jnp.bfloat16).astype(F32)
    rest = fy - top
    lhs = jnp.concatenate([jnp.transpose(jnp.concatenate([v, v], axis=0)) for v in (top, rest)], axis=1).astype(jnp.bfloat16)
    for fz in range(planes):
        y_out[fz] = pre_y[fz] - jnp.dot(lhs, back[fz], preferred_element_type=F32)

    e1, e2 = q1 * q1, q2 * q2
    close1, close2 = 1.0 / (1.0 - e1**nz), 1.0 / (1.0 - e2**nz)
    turns = nz // quarter

    def incoming(k, to):
        g1 = g2 = None
        for m in range(nz):
            shift = m + k * quarter
            v1, v2 = (pbuf[0], pbuf[1]) if m == 0 else (rb[m, 0], rb[m, 1])
            t1 = (close1 * e1 ** ((shift - 1) % nz)) * v1
            t2 = (close2 * e2 ** ((-shift - 1) % nz)) * v2
            g1, g2 = (t1, t2) if m == 0 else (g1 + t1, g2 + t2)
        to[0] = g1
        to[1] = g2

    ret = pltpu.make_async_remote_copy(gbuf, gpar, ret_s, ret_r, device_id=partner, device_id_type=MESH)

    def give(k):
        return pltpu.make_async_remote_copy(gsp.at[k - 1], gbuf, give_s, give_r,
                                            device_id=chip(k * quarter), device_id_type=MESH)

    @pl.when(ahead)
    def _():
        wait_bytes(rb.at[pl.ds(1, nz - 1)], far_r)
        incoming(0, gbuf)
        ret.start()
        for k in sorted(range(1, turns), key=lambda k: -min(k, turns - k)):
            incoming(k, gsp.at[k - 1])
            give(k).start()

    @pl.when(behind)
    def _():
        wait_bytes(gbuf, give_r)
        ret.start()

    side.wait_recv()
    a1 = jnp.where(first, 1.0, q1)
    b1 = jnp.where(first, 0.0, 1.0)
    a2 = jnp.where(first, q2, 1.0)
    b2 = jnp.where(first, 1.0, 0.0)
    f3 = jnp.where(first, fast[...], px[2])
    f4 = jnp.where(first, px[3], fast[...])
    pair.wait_send()
    side.wait_send()
    beyond[0].wait_send()
    beyond[1].wait_send()

    @pl.when(ahead)
    def _():
        wait_bytes(rb.at[pl.ds(0, quarter - 1)], far_s)

    @pl.when(behind)
    def _():
        wait_bytes(rb.at[pl.ds(0, quarter)], far_s)

    wait_bytes(yb.at[pl.ds(1, ny - 1)], ys_s)
    ret.wait_recv()
    own1, own2, par1, par2 = gbuf[0], gbuf[1], gpar[0], gpar[1]
    for h in range(2):
        mine = c == h
        f1 = a1 * jnp.where(mine, own1, par1) + b1 * px[0, h]
        f2 = a2 * jnp.where(mine, own2, par2) + b2 * px[1, h]
        for p in range(half):
            fz = h * half + p
            fix = coef[0] * f1[p:p + 1] + coef[1] * f2[p:p + 1]
            x_out[fz] = x_out[fz] - fix - coef[2] * f3[h, p:p + 1] - coef[3] * f4[h, p:p + 1]
    ret.wait_send()

    @pl.when(ahead)
    def _():
        wait_bytes(gsp, give_s)


def store_kernel(x_in, y_in, x_out, y_out, sem):
    parts = 4
    rows = x_in.shape[0] // parts
    copies = []
    for k in range(parts):
        part = pl.ds(k * rows, rows)
        copies.append(pltpu.make_async_copy(x_in.at[part], x_out.at[part], sem.at[2 * k]))
        copies.append(pltpu.make_async_copy(y_in.at[part], y_out.at[part], sem.at[2 * k + 1]))
    for copy in copies:
        copy.start()
    for copy in copies:
        copy.wait()


def on_device(fields, inv_dx, inv_dy):
    nfield, nplane, n, ncol = fields.shape
    gxn, gyn = lax.axis_size("gx"), lax.axis_size("gy")
    planes, nz = nfield * nplane, gxn // 2
    courant = float(n * gxn // 16)
    modes = line_modes(courant)
    q1, q2 = (mode[0][0] ** n for mode in modes[1:])
    half = planes // 2
    block = jax.ShapeDtypeStruct((planes, n, n), F32)
    hbm = pl.BlockSpec(memory_space=pltpu.HBM)
    vmem = pl.BlockSpec(memory_space=pltpu.VMEM)
    vm = lambda *shape: pltpu.VMEM(shape, F32)
    dma = pltpu.SemaphoreType.DMA
    x_pre, y_pre = pl.pallas_call(
        functools.partial(exchange_kernel, modes, float(q1), float(q2), nz, gyn, planes, n),
        out_shape=(pltpu.VMEM((planes, n, n), F32), pltpu.VMEM((planes, n, n), F32)),
        in_specs=[hbm] * 3,
        out_specs=(vmem, vmem),
        scratch_shapes=[
            vm(planes, n, n), vm(1, n), vm(1, n), vm(planes, n, n), vm(5, n, n), vm(4, n, n),
            pltpu.VMEM((planes, 16 * planes, n), jnp.bfloat16),
            vm(4, 2, half, n), vm(4, 2, half, n), vm(2, half, n), vm(nz, 2, half, n), vm(3, 2, half, n), vm(2, half, n), vm(2, half, n),
            vm(2, half, n), vm(4, 2, half, n), vm(gyn, 2, 2, half, n), vm(2, 2, half, n),
            dma((8,)), dma, dma, dma, dma, dma, dma, dma, dma, dma, dma, dma, dma, dma((2,)), dma((2,)),
            pltpu.SemaphoreType.REGULAR((TRACKS,)), pltpu.SemaphoreType.REGULAR((TRACKS,)), pltpu.SemaphoreType.REGULAR,
        ],
        compiler_params=pltpu.CompilerParams(
            collective_id=0, has_side_effects=True, vmem_limit_bytes=24 * 1024 * 1024),
        name="exchange",
    )(*(pltpu.with_memory_space_constraint(a, pltpu.HBM)
        for a in (fields.reshape(planes, n, n), inv_dx.reshape(1, n), inv_dy.reshape(1, n))))
    x_derivs, y_derivs = pl.pallas_call(
        store_kernel,
        out_shape=(block, block),
        in_specs=[vmem, vmem],
        out_specs=(hbm, hbm),
        scratch_shapes=[dma((8,))],
        compiler_params=pltpu.CompilerParams(vmem_limit_bytes=24 * 1024 * 1024),
        name="store",
    )(x_pre, y_pre)
    return x_derivs.reshape(fields.shape), y_derivs.reshape(fields.shape)


def solution(mesh):
    spec = P(None, None, "gx", "gy")
    return jax.shard_map(
        on_device, mesh=mesh, in_specs=(spec, P("gx"), P("gy")), out_specs=(spec, spec), check_vma=False
    )
```
